32 devices in a mesh: batch: 4 (over y, x), seq: 8 (over z, core).
Axes of the slice: x: 2, y: 2, z: 4, core: 2. Of those that a mesh axis runs over, the one named last changes fastest.
Arguments:
- tokens: bfloat16 [16, 1024, 1024], P('batch', 'seq'), may hold values from -6 to 6
- cotangent: bfloat16 [16, 1024, 1024], P('batch', 'seq'), may hold values from -6 to 6
- prenorm_gain: float32 [1024], replicated, may hold values from 0.25 to 1.75
- inproj_weight: bfloat16 [1024, 4384], P(('batch', 'seq')), may hold values from -0.1875 to 0.1875
- conv_taps: float32 [4, 2304], replicated, may hold values from -3 to 3
- conv_bias: float32 [2304], replicated, may hold values from -0.5 to 0.5
- step_bias: float32 [32], replicated, may hold values from -5.5 to -2.5
- decay_log: float32 [32], replicated, may hold values from 0 to 2.77
- skip_weight: float32 [32], replicated, may hold values from 0.5 to 1.5
- postnorm_gain: float32 [2048], replicated, may hold values from 0.25 to 1.75
- outproj_weight: bfloat16 [1024, 2048], P(('batch', 'seq')), may hold values from -0.125 to 0.125
Outputs:
- mixed: bfloat16 [16, 1024, 1024], P('batch', 'seq')
- input_grad: float32 [16, 1024, 1024], P('batch', 'seq')
- prenorm_grad: float32 [1024], replicated
- inproj_grad: float32 [1024, 4384], P(('batch', 'seq'))
- taps_grad: float32 [4, 2304], replicated
- bias_grad: float32 [2304], replicated
- step_grad: float32 [32], replicated
- decay_grad: float32 [32], replicated
- skip_grad: float32 [32], replicated
- postnorm_grad: float32 [2048], replicated
- outproj_grad: float32 [1024, 2048], P(('batch', 'seq'))
The draws below stay inside these ranges and needn't reach their ends.
All inputs are finite; a program needn't handle non-finite values.
Results may differ from the reference program's by a relative error of at most 0.012.
The reference program's roundings to bfloat16 on the way count: a program that leaves them out, or rounds other values in their place, can miss the bound.
Values may be sent and summed in bfloat16 or wider, within the bound.
A program may use at most 256 MiB of HBM per device.

```python
import jax
import jax.numpy as jnp
from jax import lax

D = 1024
HEADS = 32
HEADDIM = 64
STATE = 128
CONV = 4
BLOCK = 256
LEN = 1024
SEQUENCES = 16
INNER = 2048
PROJ = 4384
CONVCH = 2304


def block_levels(own_key, dims, split, low, top_value):
    level, own = 1.0, jax.random.fold_in(own_key, 6)
    for axis_at, blocks in split:
        heights = jnp.exp(jax.random.uniform(jax.random.fold_in(own, axis_at), (blocks,), jnp.float32, low / len(split), top_value / len(split)))
        level = level * jnp.repeat(heights, dims[axis_at] // blocks).reshape([-1 if axis == axis_at else 1 for axis in range(len(dims))])
    return level


def gaussian(rng, dims, scale, most, shards=(), kind=jnp.bfloat16):
    values = scale * jax.random.normal(rng, dims, jnp.float32)
    if shards:
        values = values * block_levels(rng, dims, shards, -0.22, 0.18)
    return jnp.clip(values, -most, most).astype(kind)


def setup_inputs(seed: int = 0) -> dict:
    seeds = jax.random.split(jax.random.key(seed), 12)
    return {
        "tokens": gaussian(seeds[0], (SEQUENCES, LEN, D), 1.0, 6.0, ((0, 4), (1, 8))),
        "cotangent": gaussian(seeds[1], (SEQUENCES, LEN, D), 1.0, 6.0, ((0, 4), (1, 8))),
        "prenorm_gain": jnp.clip(1.0 + 0.15 * jax.random.normal(seeds[2], (D,), jnp.float32), 0.25, 1.75),
        "inproj_weight": gaussian(seeds[3], (D, PROJ), D ** -0.5, 0.1875, ((0, 32),)),
        "conv_taps": gaussian(seeds[4], (CONV, CONVCH), CONV ** -0.5, 3.0, (), jnp.float32),
        "conv_bias": jnp.clip(jax.random.uniform(seeds[5], (CONVCH,), jnp.float32, -0.5, 0.5), -0.5, 0.5),
        "step_bias": jnp.clip(jax.random.uniform(seeds[6], (HEADS,), jnp.float32, -5.5, -2.5), -5.5, -2.5),
        "decay_log": jnp.clip(jax.random.uniform(seeds[7], (HEADS,), jnp.float32, 0.0, 2.77), 0.0, 2.77),
        "skip_weight": jnp.clip(jax.random.uniform(seeds[8], (HEADS,), jnp.float32, 0.5, 1.5), 0.5, 1.5),
        "postnorm_gain": jnp.clip(1.0 + 0.15 * jax.random.normal(seeds[9], (INNER,), jnp.float32), 0.25, 1.75),
        "outproj_weight": gaussian(seeds[10], (D, INNER), INNER ** -0.5, 0.125, ((0, 32),)),
    }


EPS = 1e-05
HIGH = lax.Precision.HIGHEST

@jax.custom_vjp
def low(v):
    return lax.optimization_barrier(v.astype(jnp.bfloat16)).astype(jnp.float32)

@jax.custom_vjp
def low_back(v):
    return v

def low_keep(v):
    return (low(v), None)

def low_pass(kept, grad):
    return (grad,)

def back_keep(v):
    return (v, None)

def back_low(kept, grad):
    return (low(grad),)
low.defvjp(low_keep, low_pass)
low_back.defvjp(back_keep, back_low)

def causal_filter(values, taps, bias):
    length = values.shape[0]
    padded = jnp.concatenate([jnp.zeros((taps.shape[0] - 1, values.shape[1]), jnp.float32), values], 0)
    total = jnp.zeros(values.shape, jnp.float32) + bias[None, :]
    for offset in range(taps.shape[0]):
        total = total + taps[offset][None, :] * padded[offset:offset + length]
    return total

def state_space(x_heads, dt_heads, b_rows, c_rows, decay_log, skip_weight, block):
    length, heads, width = x_heads.shape
    block_count = length // block
    rate = -jnp.exp(decay_log)
    x_blocks = x_heads.reshape(block_count, block, heads, width)
    a_blocks = (dt_heads * rate[None, :]).reshape(block_count, block, heads)
    dt_blocks = jnp.swapaxes(dt_heads.reshape(block_count, block, heads), 1, 2)
    b_blocks = b_rows.reshape(block_count, block, -1)
    c_blocks = c_rows.reshape(block_count, block, -1)
    row_ids = lax.broadcasted_iota(jnp.int32, (block, block), 0)
    col_ids = lax.broadcasted_iota(jnp.int32, (block, block), 1)
    lower = row_ids >= col_ids
    cum_decay = jnp.einsum('ij,cjh->chi', lower.astype(jnp.float32), a_blocks, precision=HIGH)
    scores = jnp.einsum('cin,cjn->cij', c_blocks, b_blocks, precision=HIGH)
    gap = cum_decay[:, :, :, None] - cum_decay[:, :, None, :]
    decay = jnp.where(lower, jnp.exp(jnp.where(lower, gap, 0.0)), 0.0)
    weights = decay * scores[:, None] * dt_blocks[:, :, None, :]
    y_diag = jnp.einsum('chij,cjhp->cihp', weights, x_blocks, precision=HIGH)
    to_end = jnp.exp(cum_decay[:, :, -1:] - cum_decay) * dt_blocks
    weighted_x = x_blocks * jnp.swapaxes(to_end, 1, 2)[..., None]
    block_state = jnp.einsum('cjn,cjhp->chnp', b_blocks, weighted_x, precision=HIGH)
    totals = cum_decay[:, :, -1]
    block_rows = lax.broadcasted_iota(jnp.int32, (block_count, block_count), 0)
    block_cols = lax.broadcasted_iota(jnp.int32, (block_count, block_count), 1)
    block_cum = jnp.einsum('kg,gh->kh', (block_rows >= block_cols).astype(jnp.float32), totals, precision=HIGH)
    entering = block_cum - totals
    before = (block_cols < block_rows)[:, :, None]
    span = entering[:, None, :] - block_cum[None, :, :]
    carry = jnp.where(before, jnp.exp(jnp.where(before, span, 0.0)), 0.0)
    start_state = jnp.einsum('kgh,ghnp->khnp', carry, block_state, precision=HIGH)
    y_off = jnp.einsum('cin,chnp->cihp', c_blocks, start_state, precision=HIGH)
    y_off = y_off * jnp.swapaxes(jnp.exp(cum_decay), 1, 2)[..., None]
    result = y_diag + y_off + skip_weight[None, None, :, None] * x_blocks
    return result.reshape(length, heads, width)

def sequence_layer(row, prenorm_gain, inproj_weight, conv_taps, conv_bias, step_bias, decay_log, skip_weight, postnorm_gain, outproj_weight):
    scale = lax.rsqrt(lax.optimization_barrier(jnp.mean(row * row, -1, keepdims=True)) + EPS)
    normed = low(row * scale * prenorm_gain)
    proj = low_back(jnp.dot(normed, inproj_weight, precision=HIGH))
    gate = proj[:, :INNER]
    x_sent = low_back(low(proj[:, INNER:2 * INNER]))
    bc_sent = low(proj[:, 2 * INNER:2 * INNER + 2 * STATE])
    step_sent = low_back(low(proj[:, 2 * INNER + 2 * STATE:]))
    x_conv = jax.nn.silu(causal_filter(x_sent, conv_taps[:, :INNER], conv_bias[:INNER]))
    bc_conv = jax.nn.silu(causal_filter(bc_sent, conv_taps[:, INNER:], conv_bias[INNER:]))
    step_heads = jax.nn.softplus(step_sent + step_bias[None, :])
    length = row.shape[0]
    y_heads = state_space(x_conv.reshape(length, HEADS, HEADDIM), step_heads, bc_conv[:, :STATE], bc_conv[:, STATE:], decay_log, skip_weight, BLOCK)
    y_sent = low_back(low(y_heads.reshape(length, INNER)))
    gated = y_sent * jax.nn.silu(gate)
    y_norm = low(gated * lax.rsqrt(lax.optimization_barrier(jnp.mean(gated * gated, -1, keepdims=True)) + EPS) * postnorm_gain)
    return row + jnp.dot(y_norm, outproj_weight.T, precision=HIGH)

def reference(tokens, cotangent, prenorm_gain, inproj_weight, conv_taps, conv_bias, step_bias, decay_log, skip_weight, postnorm_gain, outproj_weight):
    primal = (tokens.astype(jnp.float32), prenorm_gain.astype(jnp.float32), inproj_weight.astype(jnp.float32), conv_taps.astype(jnp.float32), conv_bias.astype(jnp.float32), step_bias.astype(jnp.float32), decay_log.astype(jnp.float32), skip_weight.astype(jnp.float32), postnorm_gain.astype(jnp.float32), outproj_weight.astype(jnp.float32))

    def forward(token_rows, *params):

        def single_row(row):
            return sequence_layer(row, *params)
        return lax.map(jax.checkpoint(single_row), token_rows)
    output, pullback = jax.vjp(forward, *primal)
    gradients = pullback(cotangent.astype(jnp.float32))
    return (output.astype(jnp.bfloat16), gradients[0], gradients[1], gradients[2], gradients[3], gradients[4], gradients[5], gradients[6], gradients[7], gradients[8], gradients[9])
```

```python
import functools

import jax
import jax.numpy as jnp
from jax import lax
from jax.experimental import pallas as pl
from jax.experimental.pallas import tpu as pltpu
from jax.sharding import PartitionSpec as P

HEADS = 32
HEADDIM = 64
STATE = 128
CONV = 4
INNER = 2048
PROJ = 4384
EPS = 1e-05
HIGH = lax.Precision.HIGHEST
HALO = CONV - 1
PIECE = 32


def chain_kernel(forward, local_ref, dec_ref, out_ref, sent, held, send_sem, recv_sem):
    size = lax.axis_size("seq")
    me = lax.axis_index("seq")
    up = lax.rem(me + 1, size)
    down = lax.rem(me + size - 1, size)
    target = up if forward else down
    gets = me > 0 if forward else me < size - 1
    gives = me < size - 1 if forward else me > 0
    barrier = pltpu.get_barrier_semaphore()
    for other in (up, down):
        pl.semaphore_signal(
            barrier, inc=1, device_id={"seq": other}, device_id_type=pl.DeviceIdType.MESH
        )
    pl.semaphore_wait(barrier, 2)
    seqs, states, _ = local_ref.shape
    per = states // PIECE

    def copy_of(p):
        return pltpu.make_async_remote_copy(
            src_ref=sent.at[p],
            dst_ref=held.at[p],
            send_sem=send_sem.at[p],
            recv_sem=recv_sem.at[p],
            device_id={"seq": target},
            device_id_type=pl.DeviceIdType.MESH,
        )

    def step(p, carry):
        q = p // per
        rows = pl.ds(pl.multiple_of((p % per) * PIECE, PIECE), PIECE)

        @pl.when(gets)
        def _():
            copy_of(p).wait_recv()
            out_ref[q, rows, :] = held[p]

        @pl.when(jnp.logical_not(gets))
        def _():
            out_ref[q, rows, :] = jnp.zeros((PIECE, out_ref.shape[2]), out_ref.dtype)

        @pl.when(gives)
        def _():
            value = out_ref[q, rows, :].astype(jnp.float32) * dec_ref[q] + local_ref[q, rows, :]
            sent[p] = value.astype(sent.dtype)
            copy_of(p).start()

        return carry

    lax.fori_loop(0, seqs * per, step, 0)

    @pl.when(gives)
    def _():
        def finish(p, carry):
            copy_of(p).wait_send()
            return carry

        lax.fori_loop(0, seqs * per, finish, 0)


def run_chain(local_state, dec, forward):
    seqs, states, width = local_state.shape
    pieces = seqs * (states // PIECE)
    return pl.pallas_call(
        functools.partial(chain_kernel, forward),
        out_shape=jax.ShapeDtypeStruct(local_state.shape, jnp.bfloat16),
        in_specs=[pl.BlockSpec(memory_space=pltpu.VMEM)] * 2,
        out_specs=pl.BlockSpec(memory_space=pltpu.VMEM),
        scratch_shapes=[
            pltpu.VMEM((pieces, PIECE, width), jnp.bfloat16),
            pltpu.VMEM((pieces, PIECE, width), jnp.bfloat16),
            pltpu.SemaphoreType.DMA((pieces,)),
            pltpu.SemaphoreType.DMA((pieces,)),
        ],
        compiler_params=pltpu.CompilerParams(
            collective_id=0 if forward else 1,
            has_side_effects=True,
            vmem_limit_bytes=40 * 1024 * 1024,
        ),
        name="chain_up" if forward else "chain_down",
    )(local_state, dec)


GROUP = 8
WIDE = GROUP * HEADDIM
PAIRS = GROUP // 2
BF = jnp.bfloat16
F32 = jnp.float32
LAST = (((1,), (1,)), ((), ()))
FIRST = (((0,), (0,)), ((), ()))
MIB = 1024 * 1024


def mul(a, b, dims=(((1,), (0,)), ((), ()))):
    return lax.dot_general(a, b, dims, preferred_element_type=F32)


def left_half(rows):
    return lax.broadcasted_iota(jnp.int32, (rows, 128), 1) < HEADDIM


def spread(cols, pair, sel):
    return jnp.where(sel, cols[:, 2 * pair : 2 * pair + 1], cols[:, 2 * pair + 1 : 2 * pair + 2])


def halves(v, sel):
    zero = jnp.zeros_like(v)
    return jnp.concatenate([jnp.where(sel, v, zero), jnp.where(sel, zero, v)], 0)


def conv_pre(x_ref, halo_ref, taps_ref, bias_ref, ext):
    length = x_ref.shape[0]
    ext[0:8, :] = halo_ref[0].astype(F32)
    ext[8 : 8 + length, :] = x_ref[...].astype(BF).astype(F32)
    pre = bias_ref[...]
    for k in range(CONV):
        pre = pre + taps_ref[k : k + 1, :] * ext[5 + k : 5 + k + length, :]
    return pre


def decays(cum, cum_t, head, lower):
    gap = cum[:, head : head + 1] - cum_t[head : head + 1, :]
    return jnp.where(lower, jnp.exp(gap), 0.0)


def lower_mask(length):
    return lax.broadcasted_iota(jnp.int32, (length, length), 0) >= lax.broadcasted_iota(
        jnp.int32, (length, length), 1
    )


def forward_kernel(
    x_ref, halo_ref, taps_ref, bias_ref, b_ref, c_ref, step_ref, cum_ref, cumt_ref, skip_ref,
    y_ref, state_ref, dec_ref, ext,
):
    pre = conv_pre(x_ref, halo_ref, taps_ref, bias_ref, ext)
    x = pre * jax.nn.sigmoid(pre)
    length = x.shape[0]
    b, c = b_ref[0].astype(BF), c_ref[0].astype(BF)
    scores = mul(c, b, LAST)
    lower = lower_mask(length)
    sel = left_half(length)
    step, cum, cum_t = step_ref[0, 0], cum_ref[0, 0], cumt_ref[0, 0]
    for j in range(PAIRS):
        cols = slice(128 * j, 128 * j + 128)
        xp = x[:, cols]
        xd = xp * spread(step, j, sel)
        cumx = spread(cum, j, sel)
        last = cumx[length - 1 : length, :]
        w = jnp.concatenate(
            [(scores * decays(cum, cum_t, 2 * j + i, lower)).astype(BF) for i in range(2)], 1
        )
        y_ref[0, :, cols] = mul(w, halves(xd.astype(BF), sel)) + skip_ref[:, cols] * xp
        state_ref[0, :, cols] = mul(b, (jnp.exp(last - cumx) * xd).astype(BF), FIRST)
        dec_ref[0, :, cols] = jnp.exp(last)


def finish_kernel(y_ref, start_ref, c_ref, cum_ref, gate_ref, gain_ref, sent_ref, norm_ref):
    length = y_ref.shape[1]
    sel = left_half(length)
    c = c_ref[0].astype(BF)
    squares = jnp.zeros((length, 1), F32)
    for j in range(HEADS // 2):
        cols = slice(128 * j, 128 * j + 128)
        cumx = spread(cum_ref[0], j, sel)
        y = y_ref[0, :, cols] + jnp.exp(cumx) * mul(c, start_ref[0, :, cols])
        y = y.astype(BF)
        sent_ref[:, cols] = y
        gate = gate_ref[:, cols]
        gated = y.astype(F32) * (gate * jax.nn.sigmoid(gate))
        squares = squares + jnp.sum(gated * gated, 1, keepdims=True)
    q = lax.rsqrt(squares / INNER + EPS)
    for j in range(HEADS // 2):
        cols = slice(128 * j, 128 * j + 128)
        gate = gate_ref[:, cols]
        gated = sent_ref[:, cols].astype(F32) * (gate * jax.nn.sigmoid(gate))
        norm_ref[:, cols] = (gated * q * gain_ref[:, cols]).astype(BF)


def post_kernel(
    grad_ref, sent_ref, gate_ref, gain_ref, c_ref, cum_ref,
    gate_grad_ref, y_grad_ref, gain_grad_ref, state_grad_ref,
):
    length = grad_ref.shape[0]
    sel = left_half(length)
    c = c_ref[0].astype(BF)
    squares = jnp.zeros((length, 1), F32)
    dots = jnp.zeros((length, 1), F32)
    for j in range(HEADS // 2):
        cols = slice(128 * j, 128 * j + 128)
        gate = gate_ref[:, cols]
        gated = sent_ref[:, cols].astype(F32) * (gate * jax.nn.sigmoid(gate))
        squares = squares + jnp.sum(gated * gated, 1, keepdims=True)
        dots = dots + jnp.sum(gated * grad_ref[:, cols] * gain_ref[:, cols], 1, keepdims=True)
    q = lax.rsqrt(squares / INNER + EPS)
    back = q * q * q * (dots / INNER)

    @pl.when(pl.program_id(0) == 0)
    def _():
        gain_grad_ref[...] = jnp.zeros_like(gain_grad_ref)

    for j in range(HEADS // 2):
        cols = slice(128 * j, 128 * j + 128)
        gate = gate_ref[:, cols]
        sg = jax.nn.sigmoid(gate)
        act = gate * sg
        y = sent_ref[:, cols].astype(F32)
        gated = y * act
        grad = grad_ref[:, cols]
        gain_grad_ref[:, cols] += jnp.sum(grad * gated * q, 0, keepdims=True)
        inner = q * (grad * gain_ref[:, cols]) - gated * back
        gate_grad_ref[:, cols] = (inner * y * (sg * (1.0 + gate * (1.0 - sg)))).astype(BF)
        dy = (inner * act).astype(BF)
        y_grad_ref[:, cols] = dy
        cumx = spread(cum_ref[0], j, sel)
        state_grad_ref[0, :, cols] = mul(
            c, (jnp.exp(cumx) * dy.astype(F32)).astype(BF), FIRST
        )


def backward_kernel(
    x_ref, halo_ref, taps_ref, bias_ref, b_ref, c_ref, step_ref, cum_ref, cumt_ref, skip_ref,
    dy_ref, right_ref, start_ref,
    back_ref, head_ref, stats_ref, dstep_ref, dcum_ref, dcumt_ref, db_ref, dc_ref, ext, late,
):
    pre = conv_pre(x_ref, halo_ref, taps_ref, bias_ref, ext)
    length = pre.shape[0]
    b, c = b_ref[0].astype(BF), c_ref[0].astype(BF)
    scores = mul(c, b, LAST)
    lower = lower_mask(length)
    sel = left_half(length)
    step, cum, cum_t = step_ref[0, 0], cum_ref[0, 0], cumt_ref[0, 0]
    d_scores = jnp.zeros((length, length), F32)
    db = jnp.zeros((length, STATE), F32)
    dc = jnp.zeros((length, STATE), F32)
    late[length : length + 8, :] = jnp.zeros((8, WIDE), F32)
    for j in range(PAIRS):
        cols = slice(128 * j, 128 * j + 128)
        prep = pre[:, cols]
        sg = jax.nn.sigmoid(prep)
        xp = prep * sg
        stx = spread(step, j, sel)
        xd = xp * stx
        cumx = spread(cum, j, sel)
        last = cumx[length - 1 : length, :]
        dy_low = dy_ref[:, cols]
        dy = dy_low.astype(F32)
        dy_halves = halves(dy_low, sel)
        m = mul(dy_halves, xd.astype(BF), LAST)
        weights, row_sums = [], []
        for i in range(2):
            h = 2 * j + i
            e = decays(cum, cum_t, h, lower)
            weights.append((scores * e).astype(BF))
            me = m[i * length : (i + 1) * length] * e
            d_scores = d_scores + me
            mge = me * scores
            row_sums.append(jnp.sum(mge, 1, keepdims=True))
            dcumt_ref[0, 0, h : h + 1, :] = jnp.sum(mge, 0, keepdims=True)
        ends = jnp.exp(last - cumx)
        starts = jnp.exp(cumx)
        right, start = right_ref[0, :, cols], start_ref[0, :, cols]
        b_right = ends * mul(b, right)
        dxd = mul(jnp.concatenate(weights, 0), dy_halves, FIRST) + b_right
        dy_start = starts * dy
        xd_end = b_right * xd
        moved = dy_start * mul(c, start) - xd_end
        d_st = dxd * xp
        zero = jnp.zeros_like(moved)
        for i in range(2):
            h = 2 * j + i
            keep = sel if i == 0 else jnp.logical_not(sel)
            dcum_ref[0, 0, :, h : h + 1] = row_sums[i] + jnp.sum(
                jnp.where(keep, moved, zero), 1, keepdims=True
            )
            dstep_ref[0, 0, :, h : h + 1] = jnp.sum(jnp.where(keep, d_st, zero), 1, keepdims=True)
        d_last = jnp.sum(xd_end, 0, keepdims=True) + jnp.exp(last) * jnp.sum(
            right.astype(F32) * start.astype(F32), 0, keepdims=True
        )
        dx = stx * dxd + skip_ref[:, cols] * dy
        pre_grad = dx * (sg * (1.0 + prep * (1.0 - sg)))
        late[0:length, cols] = pre_grad
        stats_ref[0, CONV : CONV + 1, cols] = jnp.sum(pre_grad, 0, keepdims=True)
        stats_ref[0, CONV + 1 : CONV + 2, cols] = jnp.sum(xp * dy, 0, keepdims=True)
        stats_ref[0, CONV + 2 : CONV + 3, cols] = d_last
        for k in range(CONV):
            stats_ref[0, k : k + 1, cols] = jnp.sum(
                pre_grad * ext[5 + k : 5 + k + length, cols], 0, keepdims=True
            )
        db = db + mul((ends * xd).astype(BF), right, LAST)
        dc = dc + mul(dy_start.astype(BF), start, LAST)
    stats_ref[0, CONV + 3 : CONV + 4, :] = jnp.zeros((1, WIDE), F32)
    low = d_scores.astype(BF)
    db = db + mul(low, c, FIRST)
    dc = dc + mul(low, b)
    first = pl.program_id(1) == 0

    @pl.when(first)
    def _():
        db_ref[0] = db
        dc_ref[0] = dc

    @pl.when(jnp.logical_not(first))
    def _():
        db_ref[0] += db
        dc_ref[0] += dc

    total = taps_ref[0:1, :] * late[HALO : HALO + length, :]
    for k in range(1, CONV):
        total = total + taps_ref[k : k + 1, :] * late[HALO - k : HALO - k + length, :]
    back_ref[...] = total
    head_ref[0] = late[0:8, :]


def causal_filter(values, taps, bias):
    length = values.shape[1] - HALO
    total = bias[None, None, :]
    for offset in range(CONV):
        total = total + taps[offset][None, None, :] * values[:, offset : offset + length]
    return total


def bc_part(values, taps, bias):
    return jax.nn.silu(causal_filter(values, taps, bias))


def step_part(sent, bias, decay_log):
    step = jax.nn.softplus(sent + bias[None, None, :])
    a = step * (-jnp.exp(decay_log))[None, None, :]
    lower = lower_mask(sent.shape[1]).astype(F32)
    return step, jnp.einsum("ij,qjh->qih", lower, a, precision=HIGH)


def params(semantics):
    return pltpu.CompilerParams(
        dimension_semantics=semantics, vmem_limit_bytes=40 * MIB
    )


def prenorm(row, gain):
    return row * lax.rsqrt(jnp.mean(row * row, -1, keepdims=True) + EPS) * gain


def local(
    tokens,
    cotangent,
    prenorm_gain,
    inproj_weight,
    conv_taps,
    conv_bias,
    step_bias,
    decay_log,
    skip_weight,
    postnorm_gain,
    outproj_weight,
):
    seqs, length, width = tokens.shape
    rows = seqs * length
    groups = HEADS // GROUP
    size = lax.axis_size("seq")
    up = [(i, i + 1) for i in range(size - 1)]
    down = [(i + 1, i) for i in range(size - 1)]
    both = ("batch", "seq")
    inproj_full = lax.all_gather(inproj_weight, both, axis=0, tiled=True)
    outproj_full = lax.all_gather(outproj_weight, both, axis=0, tiled=True)
    token_f = tokens.astype(F32)
    normed_f, pre_back = jax.vjp(prenorm, token_f, prenorm_gain)
    normed = normed_f.astype(BF).reshape(rows, width)
    proj = jnp.dot(normed, inproj_full, preferred_element_type=F32)
    by_seq = proj.reshape(seqs, length, PROJ)
    halo = lax.ppermute(
        by_seq[:, length - HALO :, INNER : 2 * INNER + 2 * STATE].astype(BF), "seq", up
    )
    halo_x = jnp.pad(halo[..., :INNER], ((0, 0), (8 - HALO, 0), (0, 0)))
    bc_sent = by_seq[..., 2 * INNER : 2 * INNER + 2 * STATE].astype(BF)
    bc_ext = jnp.concatenate([halo[..., INNER:], bc_sent], 1).astype(F32)
    bc_conv, bc_vjp = jax.vjp(bc_part, bc_ext, conv_taps[:, INNER:], conv_bias[INNER:])
    step_sent = by_seq[..., 2 * INNER + 2 * STATE :].astype(BF).astype(F32)
    (step, cum), step_vjp = jax.vjp(step_part, step_sent, step_bias, decay_log)

    def grouped(v):
        return v.reshape(seqs, length, groups, GROUP).transpose(0, 2, 1, 3)

    def ungrouped(v):
        return v.transpose(0, 2, 1, 3).reshape(seqs, length, HEADS)

    step_g, cum_g = grouped(step), grouped(cum)
    cum_t = cum.transpose(0, 2, 1).reshape(seqs, groups, GROUP, length)
    skip = jnp.repeat(skip_weight, HEADDIM)[None, :]
    bias = conv_bias[None, :]
    gain = postnorm_gain[None, :]
    offset = INNER // WIDE
    mixer_specs = [
        pl.BlockSpec((length, WIDE), lambda q, g: (q, offset + g)),
        pl.BlockSpec((1, 8, WIDE), lambda q, g: (q, 0, g)),
        pl.BlockSpec((CONV, WIDE), lambda q, g: (0, g)),
        pl.BlockSpec((1, WIDE), lambda q, g: (0, g)),
        pl.BlockSpec((1, length, STATE), lambda q, g: (q, 0, 0)),
        pl.BlockSpec((1, length, STATE), lambda q, g: (q, 0, 1)),
        pl.BlockSpec((1, 1, length, GROUP), lambda q, g: (q, g, 0, 0)),
        pl.BlockSpec((1, 1, length, GROUP), lambda q, g: (q, g, 0, 0)),
        pl.BlockSpec((1, 1, GROUP, length), lambda q, g: (q, g, 0, 0)),
        pl.BlockSpec((1, WIDE), lambda q, g: (0, g)),
    ]
    mixer_args = (
        proj, halo_x, conv_taps, bias, bc_conv, bc_conv, step_g, cum_g, cum_t, skip,
    )
    row_block = pl.BlockSpec((length, WIDE), lambda q, g: (q, g))
    state_block = pl.BlockSpec((1, STATE, WIDE), lambda q, g: (q, 0, g))

    def shape(dims, kind=F32):
        return jax.ShapeDtypeStruct(dims, kind)

    y_local, state, dec = pl.pallas_call(
        forward_kernel,
        grid=(seqs, groups),
        in_specs=mixer_specs,
        out_specs=[
            pl.BlockSpec((1, length, WIDE), lambda q, g: (q, 0, g)),
            state_block,
            pl.BlockSpec((1, 1, WIDE), lambda q, g: (q, 0, g)),
        ],
        out_shape=[
            shape((seqs, length, INNER)),
            shape((seqs, STATE, INNER)),
            shape((seqs, 1, INNER)),
        ],
        scratch_shapes=[pltpu.VMEM((length + 8, WIDE), F32)],
        compiler_params=params(("arbitrary", "arbitrary")),
        name="mixer_forward",
    )(*mixer_args)
    start = run_chain(state, dec, True)
    full_rows = pl.BlockSpec((length, INNER), lambda q: (q, 0))
    full_seq = pl.BlockSpec((1, length, INNER), lambda q: (q, 0, 0))
    full_gain = pl.BlockSpec((1, INNER), lambda q: (0, 0))
    c_block = pl.BlockSpec((1, length, STATE), lambda q: (q, 0, 1))
    cum_block = pl.BlockSpec((1, length, HEADS), lambda q: (q, 0, 0))
    y_sent, y_norm = pl.pallas_call(
        finish_kernel,
        grid=(seqs,),
        in_specs=[full_seq, full_seq, c_block, cum_block, full_rows, full_gain],
        out_specs=[full_rows, full_rows],
        out_shape=[shape((rows, INNER), BF), shape((rows, INNER), BF)],
        compiler_params=params(("arbitrary",)),
        name="mixer_finish",
    )(y_local, start, bc_conv, cum, proj, gain)
    branch = mul(y_norm, outproj_full, LAST)
    mixed = (token_f + branch.reshape(seqs, length, width)).astype(BF)
    upstream = cotangent.reshape(rows, width)
    outproj_grad = lax.psum_scatter(
        mul(upstream, y_norm, FIRST).astype(BF), both, scatter_dimension=0, tiled=True
    ).astype(F32)
    norm_grad = mul(upstream, outproj_full)
    gate_grad, y_grad, gain_grad, state_grad = pl.pallas_call(
        post_kernel,
        grid=(seqs,),
        in_specs=[full_rows, full_rows, full_rows, full_gain, c_block, cum_block],
        out_specs=[full_rows, full_rows, full_gain, full_seq],
        out_shape=[
            shape((rows, INNER), BF),
            shape((rows, INNER), BF),
            shape((1, INNER)),
            shape((seqs, STATE, INNER)),
        ],
        compiler_params=params(("arbitrary",)),
        name="post_backward",
    )(norm_grad, y_sent, proj, gain, bc_conv, cum)
    right = run_chain(state_grad, dec, False)
    back, head, stats, dstep, dcum, dcum_t, db, dc = pl.pallas_call(
        backward_kernel,
        grid=(seqs, groups),
        in_specs=mixer_specs + [row_block, state_block, state_block],
        out_specs=[
            row_block,
            pl.BlockSpec((1, 8, WIDE), lambda q, g: (q, 0, g)),
            pl.BlockSpec((1, 8, WIDE), lambda q, g: (q, 0, g)),
            pl.BlockSpec((1, 1, length, GROUP), lambda q, g: (q, g, 0, 0)),
            pl.BlockSpec((1, 1, length, GROUP), lambda q, g: (q, g, 0, 0)),
            pl.BlockSpec((1, 1, GROUP, length), lambda q, g: (q, g, 0, 0)),
            pl.BlockSpec((1, length, STATE), lambda q, g: (q, 0, 0)),
            pl.BlockSpec((1, length, STATE), lambda q, g: (q, 0, 0)),
        ],
        out_shape=[
            shape((rows, INNER)),
            shape((seqs, 8, INNER)),
            shape((seqs, 8, INNER)),
            shape((seqs, groups, length, GROUP)),
            shape((seqs, groups, length, GROUP)),
            shape((seqs, groups, GROUP, length)),
            shape((seqs, length, STATE)),
            shape((seqs, length, STATE)),
        ],
        scratch_shapes=[
            pltpu.VMEM((length + 8, WIDE), F32),
            pltpu.VMEM((length + 8, WIDE), F32),
        ],
        compiler_params=params(("arbitrary", "arbitrary")),
        name="mixer_backward",
    )(*mixer_args, y_grad, right, start)
    d_last = stats[:, CONV + 2].reshape(seqs, HEADS, HEADDIM).sum(-1)
    cum_grad = ungrouped(dcum) - dcum_t.reshape(seqs, HEADS, length).transpose(0, 2, 1)
    at_last = (jnp.arange(length) == length - 1)[None, :, None]
    cum_grad = cum_grad + jnp.where(at_last, d_last[:, None, :], 0.0)
    step_back, step_full, decay_full = step_vjp((ungrouped(dstep), cum_grad))
    bc_grad, taps_bc_grad, bias_bc_grad = bc_vjp(jnp.concatenate([db, dc], 2))
    per_channel = stats.sum(0)
    skip_full = per_channel[CONV + 1].reshape(HEADS, HEADDIM).sum(-1)
    taps_full = jnp.concatenate([per_channel[:CONV], taps_bc_grad], 1)
    bias_full = jnp.concatenate([per_channel[CONV], bias_bc_grad])
    head_x = jnp.stack(
        [
            sum(
                conv_taps[k, :INNER] * head[:, i + HALO - k - HALO]
                for k in range(CONV)
                if 0 <= i - k < HALO
            )
            for i in range(HALO)
        ],
        1,
    )
    tail = lax.ppermute(jnp.concatenate([head_x, bc_grad[:, :HALO]], 2), "seq", down)
    x_back = back.reshape(seqs, length, INNER)
    keep = length - HALO
    proj_grad = jnp.concatenate(
        [
            gate_grad.reshape(seqs, length, INNER),
            jnp.concatenate(
                [x_back[:, :keep], x_back[:, keep:] + tail[..., :INNER]], 1
            ).astype(BF),
            jnp.concatenate(
                [bc_grad[:, HALO:length], bc_grad[:, length:] + tail[..., INNER:]], 1
            ).astype(BF),
            step_back.astype(BF),
        ],
        2,
    ).reshape(rows, PROJ)
    inproj_grad = lax.psum_scatter(
        mul(normed, proj_grad, FIRST).astype(BF), both, scatter_dimension=0, tiled=True
    ).astype(F32)
    normed_grad = mul(proj_grad, inproj_full, LAST)
    token_grad, prenorm_part = pre_back(normed_grad.reshape(seqs, length, width))
    input_grad = cotangent.astype(F32) + token_grad
    summed = lax.psum(
        (prenorm_part, taps_full, bias_full, step_full, decay_full, skip_full, gain_grad[0]),
        both,
    )
    return (
        mixed,
        input_grad,
        summed[0],
        inproj_grad,
        summed[1],
        summed[2],
        summed[3],
        summed[4],
        summed[5],
        summed[6],
        outproj_grad,
    )


def solution(mesh):
    in_specs = (
        P("batch", "seq", None),
        P("batch", "seq", None),
        P(),
        P(("batch", "seq"), None),
        P(),
        P(),
        P(),
        P(),
        P(),
        P(),
        P(("batch", "seq"), None),
    )
    out_specs = (
        P("batch", "seq", None),
        P("batch", "seq", None),
        P(),
        P(("batch", "seq"), None),
        P(),
        P(),
        P(),
        P(),
        P(),
        P(),
        P(("batch", "seq"), None),
    )
    return jax.shard_map(local, mesh=mesh, in_specs=in_specs, out_specs=out_specs, check_vma=False)
```

```python
import functools

import jax
import jax.numpy as jnp
from jax import lax
from jax.experimental import pallas as pl
from jax.experimental.pallas import tpu as pltpu
from jax.sharding import PartitionSpec as P

HEADS = 32
HEADDIM = 64
STATE = 128
CONV = 4
INNER = 2048
PROJ = 4384
EPS = 1e-05
HIGH = lax.Precision.HIGHEST
HALO = CONV - 1
PIECE = 32


def chain_kernel(forward, local_ref, dec_ref, out_ref, sent, held, send_sem, recv_sem):
    size = lax.axis_size("seq")
    me = lax.axis_index("seq")
    up = lax.rem(me + 1, size)
    down = lax.rem(me + size - 1, size)
    target = up if forward else down
    gets = me > 0 if forward else me < size - 1
    gives = me < size - 1 if forward else me > 0
    barrier = pltpu.get_barrier_semaphore()
    for other in (up, down):
        pl.semaphore_signal(
            barrier, inc=1, device_id={"seq": other}, device_id_type=pl.DeviceIdType.MESH
        )
    pl.semaphore_wait(barrier, 2)
    seqs, states, _ = local_ref.shape
    per = states // PIECE

    def copy_of(p):
        return pltpu.make_async_remote_copy(
            src_ref=sent.at[p],
            dst_ref=held.at[p],
            send_sem=send_sem.at[p],
            recv_sem=recv_sem.at[p],
            device_id={"seq": target},
            device_id_type=pl.DeviceIdType.MESH,
        )

    def step(p, carry):
        q = p // per
        rows = pl.ds(pl.multiple_of((p % per) * PIECE, PIECE), PIECE)

        @pl.when(gets)
        def _():
            copy_of(p).wait_recv()
            out_ref[q, rows, :] = held[p]

        @pl.when(jnp.logical_not(gets))
        def _():
            out_ref[q, rows, :] = jnp.zeros((PIECE, out_ref.shape[2]), out_ref.dtype)

        @pl.when(gives)
        def _():
            value = out_ref[q, rows, :].astype(jnp.float32) * dec_ref[q] + local_ref[q, rows, :]
            sent[p] = value.astype(sent.dtype)
            copy_of(p).start()

        return carry

    lax.fori_loop(0, seqs * per, step, 0)

    @pl.when(gives)
    def _():
        def finish(p, carry):
            copy_of(p).wait_send()
            return carry

        lax.fori_loop(0, seqs * per, finish, 0)


def run_chain(local_state, dec, forward):
    seqs, states, width = local_state.shape
    pieces = seqs * (states // PIECE)
    return pl.pallas_call(
        functools.partial(chain_kernel, forward),
        out_shape=jax.ShapeDtypeStruct(local_state.shape, jnp.bfloat16),
        in_specs=[pl.BlockSpec(memory_space=pltpu.VMEM)] * 2,
        out_specs=pl.BlockSpec(memory_space=pltpu.VMEM),
        scratch_shapes=[
            pltpu.VMEM((pieces, PIECE, width), jnp.bfloat16),
            pltpu.VMEM((pieces, PIECE, width), jnp.bfloat16),
            pltpu.SemaphoreType.DMA((pieces,)),
            pltpu.SemaphoreType.DMA((pieces,)),
        ],
        compiler_params=pltpu.CompilerParams(
            collective_id=0 if forward else 1,
            has_side_effects=True,
            vmem_limit_bytes=40 * 1024 * 1024,
        ),
        name="chain_up" if forward else "chain_down",
    )(local_state, dec)


GROUP = 8
WIDE = GROUP * HEADDIM
PAIRS = GROUP // 2
BF = jnp.bfloat16
F32 = jnp.float32
LAST = (((1,), (1,)), ((), ()))
FIRST = (((0,), (0,)), ((), ()))
MIB = 1024 * 1024


def mul(a, b, dims=(((1,), (0,)), ((), ()))):
    return lax.dot_general(a, b, dims, preferred_element_type=F32)


def left_half(rows):
    return lax.broadcasted_iota(jnp.int32, (rows, 128), 1) < HEADDIM


def spread(cols, pair, sel):
    return jnp.where(sel, cols[:, 2 * pair : 2 * pair + 1], cols[:, 2 * pair + 1 : 2 * pair + 2])


def halves(v, sel):
    zero = jnp.zeros_like(v)
    return jnp.concatenate([jnp.where(sel, v, zero), jnp.where(sel, zero, v)], 0)


def conv_pre(x_ref, halo_ref, taps_ref, bias_ref, ext):
    length = x_ref.shape[0]
    ext[0:8, :] = halo_ref[0].astype(F32)
    ext[8 : 8 + length, :] = x_ref[...].astype(F32)
    pre = bias_ref[...]
    for k in range(CONV):
        pre = pre + taps_ref[k : k + 1, :] * ext[5 + k : 5 + k + length, :]
    return pre


def decays(cum, cum_t, head, lower):
    gap = cum[:, head : head + 1] - cum_t[head : head + 1, :]
    return jnp.where(lower, jnp.exp(gap), 0.0)


def lower_mask(length):
    return lax.broadcasted_iota(jnp.int32, (length, length), 0) >= lax.broadcasted_iota(
        jnp.int32, (length, length), 1
    )


def forward_kernel(
    x_ref, halo_ref, taps_ref, bias_ref, b_ref, c_ref, step_ref, cum_ref, cumt_ref, skip_ref,
    y_ref, state_ref, dec_ref, ext,
):
    pre = conv_pre(x_ref, halo_ref, taps_ref, bias_ref, ext)
    x = pre * jax.nn.sigmoid(pre)
    length = x.shape[0]
    b, c = b_ref[0].astype(BF), c_ref[0].astype(BF)
    scores = mul(c, b, LAST)
    lower = lower_mask(length)
    sel = left_half(length)
    step, cum, cum_t = step_ref[0, 0], cum_ref[0, 0], cumt_ref[0, 0]
    for j in range(PAIRS):
        cols = slice(128 * j, 128 * j + 128)
        xp = x[:, cols]
        xd = xp * spread(step, j, sel)
        cumx = spread(cum, j, sel)
        last = cumx[length - 1 : length, :]
        w = jnp.concatenate(
            [(scores * decays(cum, cum_t, 2 * j + i, lower)).astype(BF) for i in range(2)], 1
        )
        y_ref[0, :, cols] = mul(w, halves(xd.astype(BF), sel)) + skip_ref[:, cols] * xp
        state_ref[0, :, cols] = mul(b, (jnp.exp(last - cumx) * xd).astype(BF), FIRST)
        dec_ref[0, :, cols] = jnp.exp(last)


def finish_kernel(y_ref, start_ref, c_ref, cum_ref, gate_ref, gain_ref, sent_ref, norm_ref):
    length = y_ref.shape[1]
    sel = left_half(length)
    c = c_ref[0].astype(BF)
    squares = jnp.zeros((length, 1), F32)
    for j in range(HEADS // 2):
        cols = slice(128 * j, 128 * j + 128)
        cumx = spread(cum_ref[0], j, sel)
        y = y_ref[0, :, cols] + jnp.exp(cumx) * mul(c, start_ref[0, :, cols])
        y = y.astype(BF)
        sent_ref[:, cols] = y
        gate = gate_ref[:, cols]
        gated = y.astype(F32) * (gate * jax.nn.sigmoid(gate))
        squares = squares + jnp.sum(gated * gated, 1, keepdims=True)
    q = lax.rsqrt(squares / INNER + EPS)
    for j in range(HEADS // 2):
        cols = slice(128 * j, 128 * j + 128)
        gate = gate_ref[:, cols]
        gated = sent_ref[:, cols].astype(F32) * (gate * jax.nn.sigmoid(gate))
        norm_ref[:, cols] = (gated * q * gain_ref[:, cols]).astype(BF)


def post_kernel(
    grad_ref, sent_ref, gate_ref, gain_ref, c_ref, cum_ref,
    gate_grad_ref, y_grad_ref, gain_grad_ref, state_grad_ref,
):
    length = grad_ref.shape[0]
    sel = left_half(length)
    c = c_ref[0].astype(BF)
    squares = jnp.zeros((length, 1), F32)
    dots = jnp.zeros((length, 1), F32)
    for j in range(HEADS // 2):
        cols = slice(128 * j, 128 * j + 128)
        gate = gate_ref[:, cols]
        gated = sent_ref[:, cols].astype(F32) * (gate * jax.nn.sigmoid(gate))
        squares = squares + jnp.sum(gated * gated, 1, keepdims=True)
        dots = dots + jnp.sum(gated * grad_ref[:, cols] * gain_ref[:, cols], 1, keepdims=True)
    q = lax.rsqrt(squares / INNER + EPS)
    back = q * q * q * (dots / INNER)

    @pl.when(pl.program_id(0) == 0)
    def _():
        gain_grad_ref[...] = jnp.zeros_like(gain_grad_ref)

    for j in range(HEADS // 2):
        cols = slice(128 * j, 128 * j + 128)
        gate = gate_ref[:, cols]
        sg = jax.nn.sigmoid(gate)
        act = gate * sg
        y = sent_ref[:, cols].astype(F32)
        gated = y * act
        grad = grad_ref[:, cols]
        gain_grad_ref[:, cols] += jnp.sum(grad * gated * q, 0, keepdims=True)
        inner = q * (grad * gain_ref[:, cols]) - gated * back
        gate_grad_ref[:, cols] = (inner * y * (sg * (1.0 + gate * (1.0 - sg)))).astype(BF)
        dy = (inner * act).astype(BF)
        y_grad_ref[:, cols] = dy
        cumx = spread(cum_ref[0], j, sel)
        state_grad_ref[0, :, cols] = mul(
            c, (jnp.exp(cumx) * dy.astype(F32)).astype(BF), FIRST
        )


def backward_kernel(
    x_ref, halo_ref, taps_ref, bias_ref, b_ref, c_ref, step_ref, cum_ref, cumt_ref, skip_ref,
    dy_ref, right_ref, start_ref,
    back_ref, head_ref, edge_ref, stats_ref, dstep_ref, dcum_ref, dcumt_ref, db_ref, dc_ref, ext, late,
):
    pre = conv_pre(x_ref, halo_ref, taps_ref, bias_ref, ext)
    length = pre.shape[0]
    b, c = b_ref[0].astype(BF), c_ref[0].astype(BF)
    scores = mul(c, b, LAST)
    lower = lower_mask(length)
    sel = left_half(length)
    step, cum, cum_t = step_ref[0, 0], cum_ref[0, 0], cumt_ref[0, 0]
    d_scores = jnp.zeros((length, length), F32)
    db = jnp.zeros((length, STATE), F32)
    dc = jnp.zeros((length, STATE), F32)
    late[length : length + 8, :] = jnp.zeros((8, WIDE), F32)
    for j in range(PAIRS):
        cols = slice(128 * j, 128 * j + 128)
        prep = pre[:, cols]
        sg = jax.nn.sigmoid(prep)
        xp = prep * sg
        stx = spread(step, j, sel)
        xd = xp * stx
        cumx = spread(cum, j, sel)
        last = cumx[length - 1 : length, :]
        dy_low = dy_ref[:, cols]
        dy = dy_low.astype(F32)
        dy_halves = halves(dy_low, sel)
        m = mul(dy_halves, xd.astype(BF), LAST)
        weights, row_sums = [], []
        for i in range(2):
            h = 2 * j + i
            e = decays(cum, cum_t, h, lower)
            weights.append((scores * e).astype(BF))
            me = m[i * length : (i + 1) * length] * e
            d_scores = d_scores + me
            mge = me * scores
            row_sums.append(jnp.sum(mge, 1, keepdims=True))
            dcumt_ref[0, 0, h : h + 1, :] = jnp.sum(mge, 0, keepdims=True)
        ends = jnp.exp(last - cumx)
        starts = jnp.exp(cumx)
        right, start = right_ref[0, :, cols], start_ref[0, :, cols]
        b_right = ends * mul(b, right)
        dxd = mul(jnp.concatenate(weights, 0), dy_halves, FIRST) + b_right
        dy_start = starts * dy
        xd_end = b_right * xd
        moved = dy_start * mul(c, start) - xd_end
        d_st = dxd * xp
        zero = jnp.zeros_like(moved)
        for i in range(2):
            h = 2 * j + i
            keep = sel if i == 0 else jnp.logical_not(sel)
            dcum_ref[0, 0, :, h : h + 1] = row_sums[i] + jnp.sum(
                jnp.where(keep, moved, zero), 1, keepdims=True
            )
            dstep_ref[0, 0, :, h : h + 1] = jnp.sum(jnp.where(keep, d_st, zero), 1, keepdims=True)
        d_last = jnp.sum(xd_end, 0, keepdims=True) + jnp.exp(last) * jnp.sum(
            right.astype(F32) * start.astype(F32), 0, keepdims=True
        )
        dx = stx * dxd + skip_ref[:, cols] * dy
        pre_grad = dx * (sg * (1.0 + prep * (1.0 - sg)))
        late[0:length, cols] = pre_grad
        stats_ref[0, CONV : CONV + 1, cols] = jnp.sum(pre_grad, 0, keepdims=True)
        stats_ref[0, CONV + 1 : CONV + 2, cols] = jnp.sum(xp * dy, 0, keepdims=True)
        stats_ref[0, CONV + 2 : CONV + 3, cols] = d_last
        for k in range(CONV):
            stats_ref[0, k : k + 1, cols] = jnp.sum(
                pre_grad * ext[5 + k : 5 + k + length, cols], 0, keepdims=True
            )
        db = db + mul((ends * xd).astype(BF), right, LAST)
        dc = dc + mul(dy_start.astype(BF), start, LAST)
    stats_ref[0, CONV + 3 : CONV + 4, :] = jnp.zeros((1, WIDE), F32)
    low = d_scores.astype(BF)
    db = db + mul(low, c, FIRST)
    dc = dc + mul(low, b)
    first = pl.program_id(1) == 0

    @pl.when(first)
    def _():
        db_ref[0] = db
        dc_ref[0] = dc

    @pl.when(jnp.logical_not(first))
    def _():
        db_ref[0] += db
        dc_ref[0] += dc

    total = taps_ref[0:1, :] * late[HALO : HALO + length, :]
    for k in range(1, CONV):
        total = total + taps_ref[k : k + 1, :] * late[HALO - k : HALO - k + length, :]
    back_ref[...] = total.astype(BF)
    edge_ref[0] = total[length - 8 : length]
    head_ref[0] = late[0:8, :]


def scatter_kernel(
    part_ref, vec_ref, out_ref, all_ref,
    got_a, sum_a, got_b, sum_b, got_c, vec_a, vec_b, vec_c, own_b, own_c, *sems,
):
    send_a, recv_a, send_b, recv_b, send_c, recv_c = sems[:6]
    vsend_a, vrecv_a, vsend_b, vrecv_b, vsend_c, vrecv_c = sems[6:]
    batches, size = lax.axis_size("batch"), lax.axis_size("seq")
    pairs = size // 2
    mine, seq = lax.axis_index("batch"), lax.axis_index("seq")
    pair, core = seq // 2, seq % 2
    other = pair * 2 + 1 - core

    def batch_at(d):
        return (mine + d) % batches

    def pair_at(d):
        return (pair + d) % pairs

    def copy(src, dst, send, recv, batch, place):
        return pltpu.make_async_remote_copy(
            src_ref=src,
            dst_ref=dst,
            send_sem=send,
            recv_sem=recv,
            device_id={"batch": batch, "seq": place},
            device_id_type=pl.DeviceIdType.MESH,
        )

    partners = [(mine, other)]
    partners += [(batch_at(d), seq) for d in range(1, batches)]
    partners += [(mine, pair_at(d) * 2 + core) for d in range(1, pairs)]
    barrier = pltpu.get_barrier_semaphore()
    for batch, place in partners:
        pl.semaphore_signal(
            barrier, inc=1, device_id={"batch": batch, "seq": place},
            device_id_type=pl.DeviceIdType.MESH,
        )
    pl.semaphore_wait(barrier, len(partners))

    def first(b):
        return copy(
            part_ref.at[b, :, 1 - core], got_a.at[b], send_a.at[b], recv_a.at[b], mine, other
        )

    def second(d):
        b = batch_at(d)
        return copy(sum_a.at[b], got_b.at[mine], send_b.at[b], recv_b.at[mine], b, seq)

    def third(d):
        p = pair_at(d)
        return copy(
            sum_b.at[p], got_c.at[pair], send_c.at[p], recv_c.at[pair], mine, p * 2 + core
        )

    def vec_first():
        return copy(vec_ref, vec_a, vsend_a.at[0], vrecv_a.at[0], mine, other)

    def vec_second(d, slot):
        b = batch_at(d)
        return copy(own_b, vec_b.at[slot], vsend_b.at[b], vrecv_b.at[slot], b, seq)

    def vec_third(d, slot):
        p = pair_at(d)
        return copy(
            own_c, vec_c.at[slot], vsend_c.at[p], vrecv_c.at[slot], mine, p * 2 + core
        )

    order = list(range(1, batches)) + [0]
    vec_first().start()
    for d in order:
        first(batch_at(d)).start()
    vec_first().wait_recv()
    own_b[...] = vec_ref[...] + vec_a[...]
    vec_b[mine] = own_b[...]
    for d in range(1, batches):
        vec_second(d, mine).start()
    for d in order:
        b = batch_at(d)
        first(b).wait_recv()

        def add_a(p, carry):
            sum_a[b, p] = (
                part_ref[b, p, core].astype(F32) + got_a[b, p].astype(F32)
            ).astype(BF)
            return carry

        lax.fori_loop(0, pairs, add_a, 0)
        if d:
            second(d).start()
    for d in range(1, batches):
        b = batch_at(d)
        copy(sum_a.at[b], got_b.at[b], send_b.at[b], recv_b.at[b], b, seq).wait_recv()
    for d in range(1, batches):
        vec_second(d, batch_at(d)).wait_recv()
    vec = vec_b[0]
    for b in range(1, batches):
        vec = vec + vec_b[b]
    own_c[...] = vec
    vec_c[pair] = vec
    for d in range(1, pairs):
        vec_third(d, pair).start()
    for d in list(range(1, pairs)) + [0]:
        p = pair_at(d)
        total = sum_a[mine, p].astype(F32)
        for e in range(1, batches):
            total = total + got_b[batch_at(e), p].astype(F32)
        if d:
            sum_b[p] = total.astype(BF)
            third(d).start()
    for d in range(1, pairs):
        p = pair_at(d)
        copy(
            sum_b.at[p], got_c.at[p], send_c.at[p], recv_c.at[p], mine, p * 2 + core
        ).wait_recv()
        total = total + got_c[p].astype(F32)
    out_ref[...] = total
    for d in range(1, pairs):
        vec_third(d, pair_at(d)).wait_recv()
    vec = vec_c[0]
    for p in range(1, pairs):
        vec = vec + vec_c[p]
    all_ref[...] = vec
    vec_first().wait_send()
    for d in range(1, batches):
        vec_second(d, mine).wait_send()
    for d in range(1, pairs):
        vec_third(d, pair).wait_send()
    for d in order:
        first(batch_at(d)).wait_send()
    for d in range(1, batches):
        second(d).wait_send()
    for d in range(1, pairs):
        third(d).wait_send()


def scatter_sum(part, vec):
    both = ("batch", "seq")
    batches, size = lax.axis_size("batch"), lax.axis_size("seq")
    total, width = part.shape
    rows = total // (batches * size)
    if rows % 16 or size % 2:
        rows_sum = lax.psum_scatter(part, both, scatter_dimension=0, tiled=True)
        return rows_sum.astype(F32), lax.psum(vec, both)
    pairs = size // 2
    sems = [n for n in (batches, batches, pairs, 1, batches, pairs) for _ in range(2)]
    return pl.pallas_call(
        scatter_kernel,
        out_shape=[
            jax.ShapeDtypeStruct((rows, width), F32),
            jax.ShapeDtypeStruct(vec.shape, F32),
        ],
        in_specs=[pl.BlockSpec(memory_space=pltpu.VMEM)] * 2,
        out_specs=[pl.BlockSpec(memory_space=pltpu.VMEM)] * 2,
        scratch_shapes=[
            pltpu.VMEM((batches, pairs, rows, width), BF),
            pltpu.VMEM((batches, pairs, rows, width), BF),
            pltpu.VMEM((batches, pairs, rows, width), BF),
            pltpu.VMEM((pairs, rows, width), BF),
            pltpu.VMEM((pairs, rows, width), BF),
            pltpu.VMEM(vec.shape, F32),
            pltpu.VMEM((batches,) + vec.shape, F32),
            pltpu.VMEM((pairs,) + vec.shape, F32),
            pltpu.VMEM(vec.shape, F32),
            pltpu.VMEM(vec.shape, F32),
        ]
        + [pltpu.SemaphoreType.DMA((n,)) for n in sems],
        compiler_params=pltpu.CompilerParams(
            collective_id=2, has_side_effects=True, vmem_limit_bytes=48 * MIB
        ),
        name="scatter_sum",
    )(part.reshape(batches, pairs, 2, rows, width), vec)


def causal_filter(values, taps, bias):
    length = values.shape[1] - HALO
    total = bias[None, None, :]
    for offset in range(CONV):
        total = total + taps[offset][None, None, :] * values[:, offset : offset + length]
    return total


def bc_part(values, taps, bias):
    return jax.nn.silu(causal_filter(values, taps, bias))


def step_part(sent, bias, decay_log):
    step = jax.nn.softplus(sent + bias[None, None, :])
    a = step * (-jnp.exp(decay_log))[None, None, :]
    lower = lower_mask(sent.shape[1]).astype(F32)
    return step, jnp.einsum("ij,qjh->qih", lower, a, precision=HIGH)


def params(semantics):
    return pltpu.CompilerParams(
        dimension_semantics=semantics, vmem_limit_bytes=40 * MIB
    )


def prenorm(row, gain):
    return row * lax.rsqrt(jnp.mean(row * row, -1, keepdims=True) + EPS) * gain


def local(
    tokens,
    cotangent,
    prenorm_gain,
    inproj_weight,
    conv_taps,
    conv_bias,
    step_bias,
    decay_log,
    skip_weight,
    postnorm_gain,
    outproj_weight,
):
    seqs, length, width = tokens.shape
    rows = seqs * length
    groups = HEADS // GROUP
    size = lax.axis_size("seq")
    up = [(i, i + 1) for i in range(size - 1)]
    down = [(i + 1, i) for i in range(size - 1)]
    both = ("batch", "seq")
    inproj_full = lax.all_gather(inproj_weight, both, axis=0, tiled=True)
    inproj_full, outproj_later = lax.optimization_barrier((inproj_full, outproj_weight))
    outproj_full = lax.all_gather(outproj_later, both, axis=0, tiled=True)
    token_f = tokens.astype(F32)
    normed_f, pre_back = jax.vjp(prenorm, token_f, prenorm_gain)
    normed = normed_f.astype(BF).reshape(rows, width)
    small = 2 * INNER
    weights_gate = inproj_full[:, :INNER]
    weights_x = inproj_full[:, INNER:small]
    weights_rest = inproj_full[:, small:]
    gate = mul(normed, weights_gate)
    x_raw = mul(normed, weights_x).astype(BF)
    rest = mul(normed, weights_rest).astype(BF).reshape(seqs, length, PROJ - small)
    x_seq = x_raw.reshape(seqs, length, INNER)
    halo = lax.ppermute(
        jnp.concatenate(
            [x_seq[:, length - HALO :], rest[:, length - HALO :, : 2 * STATE]], 2
        ),
        "seq",
        up,
    )
    halo_x = jnp.pad(halo[..., :INNER], ((0, 0), (8 - HALO, 0), (0, 0)))
    bc_sent = rest[..., : 2 * STATE]
    bc_ext = jnp.concatenate([halo[..., INNER:], bc_sent], 1).astype(F32)
    bc_conv, bc_vjp = jax.vjp(bc_part, bc_ext, conv_taps[:, INNER:], conv_bias[INNER:])
    step_sent = rest[..., 2 * STATE :].astype(F32)
    (step, cum), step_vjp = jax.vjp(step_part, step_sent, step_bias, decay_log)

    def grouped(v):
        return v.reshape(seqs, length, groups, GROUP).transpose(0, 2, 1, 3)

    def ungrouped(v):
        return v.transpose(0, 2, 1, 3).reshape(seqs, length, HEADS)

    step_g, cum_g = grouped(step), grouped(cum)
    cum_t = cum.transpose(0, 2, 1).reshape(seqs, groups, GROUP, length)
    skip = jnp.repeat(skip_weight, HEADDIM)[None, :]
    bias = conv_bias[None, :]
    gain = postnorm_gain[None, :]
    mixer_specs = [
        pl.BlockSpec((length, WIDE), lambda q, g: (q, g)),
        pl.BlockSpec((1, 8, WIDE), lambda q, g: (q, 0, g)),
        pl.BlockSpec((CONV, WIDE), lambda q, g: (0, g)),
        pl.BlockSpec((1, WIDE), lambda q, g: (0, g)),
        pl.BlockSpec((1, length, STATE), lambda q, g: (q, 0, 0)),
        pl.BlockSpec((1, length, STATE), lambda q, g: (q, 0, 1)),
        pl.BlockSpec((1, 1, length, GROUP), lambda q, g: (q, g, 0, 0)),
        pl.BlockSpec((1, 1, length, GROUP), lambda q, g: (q, g, 0, 0)),
        pl.BlockSpec((1, 1, GROUP, length), lambda q, g: (q, g, 0, 0)),
        pl.BlockSpec((1, WIDE), lambda q, g: (0, g)),
    ]
    mixer_args = (
        x_raw, halo_x, conv_taps, bias, bc_conv, bc_conv, step_g, cum_g, cum_t, skip,
    )
    row_block = pl.BlockSpec((length, WIDE), lambda q, g: (q, g))
    state_block = pl.BlockSpec((1, STATE, WIDE), lambda q, g: (q, 0, g))

    def shape(dims, kind=F32):
        return jax.ShapeDtypeStruct(dims, kind)

    y_local, state, dec = pl.pallas_call(
        forward_kernel,
        grid=(seqs, groups),
        in_specs=mixer_specs,
        out_specs=[
            pl.BlockSpec((1, length, WIDE), lambda q, g: (q, 0, g)),
            state_block,
            pl.BlockSpec((1, 1, WIDE), lambda q, g: (q, 0, g)),
        ],
        out_shape=[
            shape((seqs, length, INNER)),
            shape((seqs, STATE, INNER)),
            shape((seqs, 1, INNER)),
        ],
        scratch_shapes=[pltpu.VMEM((length + 8, WIDE), F32)],
        compiler_params=params(("arbitrary", "arbitrary")),
        name="mixer_forward",
    )(*mixer_args)
    start = run_chain(state, dec, True)
    full_rows = pl.BlockSpec((length, INNER), lambda q: (q, 0))
    full_seq = pl.BlockSpec((1, length, INNER), lambda q: (q, 0, 0))
    full_gain = pl.BlockSpec((1, INNER), lambda q: (0, 0))
    c_block = pl.BlockSpec((1, length, STATE), lambda q: (q, 0, 1))
    cum_block = pl.BlockSpec((1, length, HEADS), lambda q: (q, 0, 0))
    y_sent, y_norm = pl.pallas_call(
        finish_kernel,
        grid=(seqs,),
        in_specs=[full_seq, full_seq, c_block, cum_block, full_rows, full_gain],
        out_specs=[full_rows, full_rows],
        out_shape=[shape((rows, INNER), BF), shape((rows, INNER), BF)],
        compiler_params=params(("arbitrary",)),
        name="mixer_finish",
    )(y_local, start, bc_conv, cum, gate, gain)
    branch = mul(y_norm, outproj_full, LAST)
    mixed = (token_f + branch.reshape(seqs, length, width)).astype(BF)
    upstream = cotangent.reshape(rows, width)
    norm_grad = mul(upstream, outproj_full)
    gate_grad, y_grad, gain_grad, state_grad = pl.pallas_call(
        post_kernel,
        grid=(seqs,),
        in_specs=[full_rows, full_rows, full_rows, full_gain, c_block, cum_block],
        out_specs=[full_rows, full_rows, full_gain, full_seq],
        out_shape=[
            shape((rows, INNER), BF),
            shape((rows, INNER), BF),
            shape((1, INNER)),
            shape((seqs, STATE, INNER)),
        ],
        compiler_params=params(("arbitrary",)),
        name="post_backward",
    )(norm_grad, y_sent, gate, gain, bc_conv, cum)
    right = run_chain(state_grad, dec, False)
    right, y_late, gate_late = lax.optimization_barrier((right, y_norm, gate_grad))
    early = jnp.concatenate(
        [mul(upstream, y_late, FIRST).astype(BF), mul(normed, gate_late, FIRST).astype(BF)], 1
    )
    early = lax.psum_scatter(early, both, scatter_dimension=0, tiled=True).astype(F32)
    outproj_grad = early[:, :INNER]
    back, head, edge, stats, dstep, dcum, dcum_t, db, dc = pl.pallas_call(
        backward_kernel,
        grid=(seqs, groups),
        in_specs=mixer_specs + [row_block, state_block, state_block],
        out_specs=[
            row_block,
            pl.BlockSpec((1, 8, WIDE), lambda q, g: (q, 0, g)),
            pl.BlockSpec((1, 8, WIDE), lambda q, g: (q, 0, g)),
            pl.BlockSpec((1, 8, WIDE), lambda q, g: (q, 0, g)),
            pl.BlockSpec((1, 1, length, GROUP), lambda q, g: (q, g, 0, 0)),
            pl.BlockSpec((1, 1, length, GROUP), lambda q, g: (q, g, 0, 0)),
            pl.BlockSpec((1, 1, GROUP, length), lambda q, g: (q, g, 0, 0)),
            pl.BlockSpec((1, length, STATE), lambda q, g: (q, 0, 0)),
            pl.BlockSpec((1, length, STATE), lambda q, g: (q, 0, 0)),
        ],
        out_shape=[
            shape((rows, INNER), BF),
            shape((seqs, 8, INNER)),
            shape((seqs, 8, INNER)),
            shape((seqs, 8, INNER)),
            shape((seqs, groups, length, GROUP)),
            shape((seqs, groups, length, GROUP)),
            shape((seqs, groups, GROUP, length)),
            shape((seqs, length, STATE)),
            shape((seqs, length, STATE)),
        ],
        scratch_shapes=[
            pltpu.VMEM((length + 8, WIDE), F32),
            pltpu.VMEM((length + 8, WIDE), F32),
        ],
        compiler_params=params(("arbitrary", "arbitrary")),
        name="mixer_backward",
    )(*mixer_args, y_grad, right, start)
    d_last = stats[:, CONV + 2].reshape(seqs, HEADS, HEADDIM).sum(-1)
    cum_grad = ungrouped(dcum) - dcum_t.reshape(seqs, HEADS, length).transpose(0, 2, 1)
    at_last = (jnp.arange(length) == length - 1)[None, :, None]
    cum_grad = cum_grad + jnp.where(at_last, d_last[:, None, :], 0.0)
    step_back, step_full, decay_full = step_vjp((ungrouped(dstep), cum_grad))
    bc_grad, taps_bc_grad, bias_bc_grad = bc_vjp(jnp.concatenate([db, dc], 2))
    per_channel = stats.sum(0)
    skip_full = per_channel[CONV + 1].reshape(HEADS, HEADDIM).sum(-1)
    taps_full = jnp.concatenate([per_channel[:CONV], taps_bc_grad], 1)
    bias_full = jnp.concatenate([per_channel[CONV], bias_bc_grad])
    head_x = jnp.stack(
        [
            sum(
                conv_taps[k, :INNER] * head[:, i + HALO - k - HALO]
                for k in range(CONV)
                if 0 <= i - k < HALO
            )
            for i in range(HALO)
        ],
        1,
    )
    tail = lax.ppermute(jnp.concatenate([head_x, bc_grad[:, :HALO]], 2), "seq", down)
    x_edge = (edge[:, 8 - HALO :] + tail[..., :INNER]).astype(BF)
    x_back = lax.dynamic_update_slice(
        back.reshape(seqs, length, INNER), x_edge, (0, length - HALO, 0)
    ).reshape(rows, INNER)
    rest_back = jnp.concatenate(
        [
            jnp.concatenate(
                [bc_grad[:, HALO:length], bc_grad[:, length:] + tail[..., INNER:]], 1
            ),
            step_back,
        ],
        2,
    ).astype(BF).reshape(rows, PROJ - small)
    normed_grad = (
        mul(gate_grad, weights_gate, LAST)
        + mul(x_back, weights_x, LAST)
        + mul(rest_back, weights_rest, LAST)
    )
    token_grad, prenorm_part = pre_back(normed_grad.reshape(seqs, length, width))
    input_grad = cotangent.astype(F32) + token_grad
    vectors = (
        prenorm_part, taps_full, bias_full, step_full, decay_full, skip_full, gain_grad[0]
    )
    packed = jnp.concatenate([v.reshape(-1) for v in vectors])
    packed = jnp.pad(packed, (0, -packed.size % 1024)).reshape(8, -1)
    late_sum, flat = scatter_sum(
        jnp.concatenate(
            [mul(normed, x_back, FIRST).astype(BF), mul(normed, rest_back, FIRST).astype(BF)], 1
        ),
        packed,
    )
    inproj_grad = jnp.concatenate([early[:, INNER:], late_sum], 1)
    flat = flat.reshape(-1)
    summed, at = [], 0
    for v in vectors:
        summed.append(flat[at : at + v.size].reshape(v.shape))
        at += v.size
    return (
        mixed,
        input_grad,
        summed[0],
        inproj_grad,
        *summed[1:],
        outproj_grad,
    )


def solution(mesh):
    in_specs = (
        P("batch", "seq", None),
        P("batch", "seq", None),
        P(),
        P(("batch", "seq"), None),
        P(),
        P(),
        P(),
        P(),
        P(),
        P(),
        P(("batch", "seq"), None),
    )
    out_specs = (
        P("batch", "seq", None),
        P("batch", "seq", None),
        P(),
        P(("batch", "seq"), None),
        P(),
        P(),
        P(),
        P(),
        P(),
        P(),
        P(("batch", "seq"), None),
    )
    return jax.shard_map(local, mesh=mesh, in_specs=in_specs, out_specs=out_specs, check_vma=False)
```
